32 devices in a mesh: row: 4 (over y, x), col: 2 (over core), layer: 4 (over z).
Axes of the slice: x: 2, y: 2, z: 4, core: 2. Of those that a mesh axis runs over, the one named last changes fastest.
Arguments:
- a_blocks: bfloat16 [4, 2, 16, 64, 512], P('layer', None, ('row', 'col')), may hold values from -0.09375 to 0.09375
- a_cols: int32 [4, 2, 16, 8], P('layer', None, ('row', 'col')), may hold values from 0 to 7
- p_blocks: bfloat16 [4, 2, 2, 8, 64, 256], P('layer', None, 'col', 'row'), may hold values from -12 to 12
- p_cols: int32 [4, 2, 2, 8, 4], P('layer', None, 'col', 'row'), may hold values from 0 to 15, as said below
- c_cols: int32 [2, 16, 8], P('col', 'row'), may hold values from 0 to 15, as said below
Outputs:
- c_blocks: bfloat16 [2, 16, 64, 512], P('col', ('row', 'layer'))
The draws below stay inside these ranges and needn't reach their ends.
Inputs may be any that keep to these rules, and one draw needn't show every extreme that they name: `p_cols`: the 4 entries of a block row of P in one column group are distinct. `c_cols`: the 8 entries of a block row of C in one column group are distinct.
All inputs are finite; a program needn't handle non-finite values.
Results may differ from the reference program's by a relative error of at most 0.008.
Values may be sent and summed in bfloat16 or wider, within the bound.
A program may use at most 64 MiB of HBM per device.

```python
import jax
import jax.numpy as jnp
from jax import lax

BLK = 64
KS = 8
KP = 4
KC = 8
NCC = 16
SECTIONS = 2
LAYERS = 4
GROUPS = 2
RB_ALL = 16
IBS = 8


def pick_distinct(key, leading, width, wanted):
    scores = jax.random.randint(key, leading + (width,), 0, 4096) * width + jnp.arange(width, dtype=jnp.int32)
    order = jnp.argsort(scores, axis=-1)
    return order[..., :wanted].astype(jnp.int32)


def draw_p_cols(key, part):
    return pick_distinct(jax.random.fold_in(key, 11), (LAYERS, SECTIONS, GROUPS, IBS), NCC, KP)


def draw_c_cols(key, part):
    return pick_distinct(jax.random.fold_in(key, 23), (GROUPS, RB_ALL), NCC, KC)


def set_ends(values, own_key, least, largest):
    spot = [jax.random.randint(jax.random.fold_in(own_key, axis), (), 0, length) for axis, length in enumerate(values.shape)]
    widest = values.shape.index(max(values.shape))
    next_to = spot[:widest] + [(spot[widest] + 1) % values.shape[widest]] + spot[widest + 1:]
    return values.at[tuple(spot)].set(least).at[tuple(next_to)].set(largest)


def steps_of(own_key, dims, cuts, low, top_value):
    gain = 1.0
    for position, shards_of in cuts:
        draws = jax.random.uniform(jax.random.fold_in(jax.random.fold_in(own_key, 6), position), (shards_of,), jnp.float32, low / len(cuts), top_value / len(cuts))
        gain = gain * jnp.repeat(jnp.exp(draws), dims[position] // shards_of).reshape((-1,) + (1,) * (len(dims) - 1 - position))
    return gain


def noise(stream_key, extent, spread, most, shards=(), kind=jnp.bfloat16):
    array = jax.random.normal(stream_key, extent, jnp.float32) * spread
    if len(shards) > 0:
        array = steps_of(stream_key, extent, shards, -0.22, 0.18) * array
    return jnp.clip(array, min=-most, max=most).astype(kind)


def setup_inputs(seed: int = 0) -> dict:
    streams_of = jax.random.split(jax.random.key(seed), 6)
    return {
        "a_blocks": noise(streams_of[0], (LAYERS, SECTIONS, RB_ALL, BLK, KS * BLK), (BLK * KS * SECTIONS * LAYERS) ** -0.5, 0.09375, ((0, 4), (2, 8))),
        "a_cols": set_ends(jax.random.randint(streams_of[1], (LAYERS, SECTIONS, RB_ALL, KS), 0, IBS), jax.random.fold_in(streams_of[1], 1), 0, IBS - 1).astype(jnp.int32),
        "p_blocks": noise(streams_of[2], (LAYERS, SECTIONS, GROUPS, IBS, BLK, KP * BLK), 2.0, 12.0, ((0, 4), (2, 2), (3, 4))),
        "p_cols": draw_p_cols(jax.random.fold_in(streams_of[5], 71), 0),
        "c_cols": draw_c_cols(jax.random.fold_in(streams_of[5], 71), 0),
    }


def reference(a_blocks, a_cols, p_blocks, p_cols, c_cols):
    a_flat = a_blocks.reshape(LAYERS * SECTIONS, RB_ALL, BLK, KS * BLK)
    idx_flat = a_cols.reshape(LAYERS * SECTIONS, RB_ALL, KS)

    def one_group(inputs):
        p_group, pc_group, targets = inputs
        p_flat = p_group.reshape(LAYERS * SECTIONS, IBS, BLK, KP * BLK)
        pc_flat = pc_group.reshape(LAYERS * SECTIONS, IBS, KP)

        def advance(running, pieces):
            a_strip, row_idx, p_panel, panel_idx = pieces
            picked = p_panel[row_idx].astype(jnp.float32)
            a_four = a_strip.astype(jnp.float32).reshape(RB_ALL, BLK, KS, BLK)
            prods = jnp.einsum('ixky,ikyz->ikxz', a_four, picked).reshape(RB_ALL, KS, BLK, KP, BLK)
            coarse = panel_idx[row_idx]
            onehot = (coarse[:, :, :, None] == targets[:, None, None, :]).astype(jnp.float32)
            placed = jnp.einsum('ikxjz,ikjm->ixmz', prods, onehot).reshape(RB_ALL, BLK, KC * BLK)
            return running + placed, None

        start_acc = jnp.zeros((RB_ALL, BLK, KC * BLK), jnp.float32)
        summed, _ = lax.scan(advance, start_acc, (a_flat, idx_flat, p_flat, pc_flat))
        return summed.astype(jnp.bfloat16)

    return lax.map(one_group, (jnp.moveaxis(p_blocks, 2, 0), jnp.moveaxis(p_cols, 2, 0), c_cols))
```

```python
import functools

import jax
import jax.numpy as jnp
from jax import lax
from jax.experimental import pallas as pl
from jax.experimental.pallas import tpu as pltpu
from jax.sharding import PartitionSpec as P

MESH = pl.DeviceIdType.MESH
LANES = 128
NCC = 16


def partner(me, d, n):
    out = 0
    bit = 1
    while bit < n:
        out = out + lax.rem(lax.div(me, bit) + ((d // bit) % 2), 2) * bit
        bit *= 2
    return out


def pair_codes(values, half):
    lane = lax.broadcasted_iota(jnp.int32, (1, LANES), 1)
    low = lane < half
    codes = []
    for p in range(len(values) // 2):
        codes.append(jnp.where(low, values[2 * p], values[2 * p + 1]))
        codes.append(jnp.where(low, values[2 * p + 1], values[2 * p]))
    return codes


def pair_tiles(x, half):
    tiles = []
    for p in range(x.shape[1] // LANES):
        tile = x[:, p * LANES:(p + 1) * LANES].astype(jnp.float32)
        tiles.append(tile)
        tiles.append(pltpu.roll(tile, half, axis=1))
    return tiles


def kernel(dims, a_hbm, a_cols, p_hbm, p_cols, c_cols, out_ref,
           a_v, p_all, code_all, at_all, spread, t_acc, t_pick, own, c_send, c_recv,
           in_sem, ps, pr, cs, cr, as_, ar, zs, zr):
    n_row, n_col, n_layer = dims
    sections, rl, side, width = a_v.shape
    rp = p_all.shape[2]
    group = at_all.shape[0] * rl
    own_rows = c_send.shape[1]
    kc = c_cols.shape[2]
    my_row, my_col, my_layer = (lax.axis_index(x) for x in ("row", "col", "layer"))

    barrier = pltpu.get_barrier_semaphore()
    for axis, me, n in (("row", my_row, n_row), ("col", my_col, n_col), ("layer", my_layer, n_layer)):
        for d in range(1, n):
            pl.semaphore_signal(barrier, inc=1, device_id={axis: partner(me, d, n)}, device_id_type=MESH)

    load_p = pltpu.make_async_copy(p_hbm.at[0, :, 0], p_all.at[my_row], in_sem.at[0])
    load_a = pltpu.make_async_copy(a_hbm.at[0], a_v, in_sem.at[1])
    load_p.start()
    load_a.start()

    lane = lax.broadcasted_iota(jnp.int32, (side, LANES), 1)
    low = lane < side
    second = jnp.where(low, 0, 1)

    per_row = p_cols.shape[4]
    for s in range(sections):
        for r in range(rp):
            codes = pair_codes([p_cols[0, s, 0, r, j] for j in range(per_row)], side)
            for v, code in enumerate(codes):
                at = (s * rp + r) * per_row + v
                code_all[my_row, at:at + 1, :] = code

    load_a.wait()
    for s in range(sections):
        for i in range(rl):
            codes = pair_codes([a_cols[0, s, i, k] for k in range(width // side)], side)
            codes = [jnp.broadcast_to(code, (side, LANES)) for code in codes]
            tiles = pair_tiles(a_v[s, i], side)
            for q in range(n_row * rp // 2):
                total = jnp.zeros((side, LANES), jnp.float32)
                for code, tile in zip(codes, tiles):
                    total = total + jnp.where(code == 2 * q + second, tile, 0.0)
                slot = 2 * q // rp
                start = (s * rp + 2 * q % rp) * side
                at_all[my_col, slot, i * side:(i + 1) * side, start:start + LANES] = total.astype(jnp.bfloat16)

    load_p.wait()
    pl.semaphore_wait(barrier, (n_row - 1) + (n_col - 1) + (n_layer - 1))

    sends = []
    p_copies, a_copies = [], []
    for d in range(1, n_row):
        to = {"row": partner(my_row, d, n_row)}
        code_copy = pltpu.make_async_remote_copy(
            code_all.at[my_row], code_all.at[my_row], cs.at[d - 1], cr.at[d - 1], device_id=to, device_id_type=MESH)
        code_copy.start()
        copy = pltpu.make_async_remote_copy(
            p_all.at[my_row], p_all.at[my_row], ps.at[d - 1], pr.at[d - 1], device_id=to, device_id_type=MESH)
        copy.start()
        p_copies.append((code_copy, copy))
        sends += [code_copy, copy]
    for d in range(1, n_col):
        copy = pltpu.make_async_remote_copy(
            at_all.at[my_col], at_all.at[my_col], as_.at[d - 1], ar.at[d - 1],
            device_id={"col": partner(my_col, d, n_col)}, device_id_type=MESH)
        copy.start()
        a_copies.append(copy)
        sends.append(copy)

    def spread_rows(slot, to):
        for s in range(sections):
            for r in range(rp):
                codes = []
                for v in range(per_row):
                    at = (s * rp + r) * per_row + v
                    codes.append(jnp.broadcast_to(code_all[slot, at:at + 1, :], (side, LANES)))
                tiles = pair_tiles(p_all[slot, s, r], side)
                for q in range(NCC // 2):
                    total = jnp.zeros((side, LANES), jnp.float32)
                    for code, tile in zip(codes, tiles):
                        total = jnp.where(code == 2 * q + second, tile, total)
                    first = (s * rp + r) * side
                    spread[to, first:first + side, q * LANES:(q + 1) * LANES] = total.astype(jnp.bfloat16)

    step_cols = 2 * LANES
    for d in range(n_row):
        slot = partner(my_row, d, n_row)
        if d > 0:
            for copy in p_copies[d - 1]:
                copy.wait_recv()
        spread_rows(slot, d)
        if d == 0:
            for copy in a_copies:
                copy.wait_recv()
        left = at_all[:, slot].reshape(group * side, sections * rp * side)
        for n in range(0, NCC * side, step_cols):
            part = jnp.dot(left, spread[d, :, n:n + step_cols], preferred_element_type=jnp.float32)
            if d > 0:
                part = part + t_acc[:, n:n + step_cols]
            if d < n_row - 1:
                t_acc[:, n:n + step_cols] = part
            else:
                for i in range(group):
                    for h in range(step_cols // LANES):
                        tile = part[i * side:(i + 1) * side, h * LANES:(h + 1) * LANES]
                        q = n // LANES + h
                        t_pick[i, q] = tile
                        t_pick[i, NCC // 2 + q] = pltpu.roll(tile, side, axis=1)

    def pick(i, u):
        c0 = c_cols[0, i, 2 * u]
        c1 = c_cols[0, i, 2 * u + 1]
        at0 = lax.rem(c0, 2) * (NCC // 2) + lax.div(c0, 2)
        at1 = (1 - lax.rem(c1, 2)) * (NCC // 2) + lax.div(c1, 2)
        return jnp.where(low, t_pick[i, at0], t_pick[i, at1])

    z_copies = []
    for d in range(n_layer - 1, 0, -1):
        dst = partner(my_layer, d, n_layer)
        for o in range(own_rows):
            for u in range(kc // 2):
                c_send[d - 1, o, :, u * LANES:(u + 1) * LANES] = pick(dst * own_rows + o, u).astype(jnp.bfloat16)
        copy = pltpu.make_async_remote_copy(
            c_send.at[d - 1], c_recv.at[d - 1], zs.at[d - 1], zr.at[d - 1],
            device_id={"layer": dst}, device_id_type=MESH)
        copy.start()
        z_copies.append(copy)
        sends.append(copy)
    for o in range(own_rows):
        for u in range(kc // 2):
            own[o, :, u * LANES:(u + 1) * LANES] = pick(my_layer * own_rows + o, u)
    for copy in reversed(z_copies):
        copy.wait_recv()
    total = own[...]
    for d in range(1, n_layer):
        total = total + c_recv[d - 1].astype(jnp.float32)
    out_ref[0] = total.astype(jnp.bfloat16)
    for copy in sends:
        copy.wait_send()


def local(dims, a_blocks, a_cols, p_blocks, p_cols, c_cols):
    n_row, n_col, n_layer = dims
    sections, rl, side, width = a_blocks.shape[1:]
    rp, p_width = p_blocks.shape[3], p_blocks.shape[5]
    group, kc = c_cols.shape[1:]
    own_rows = group // n_layer
    codes = sections * rp * (p_width // side)
    strip = (own_rows, side, kc * side)
    depth = sections * rp * side
    dma = pltpu.SemaphoreType.DMA
    return pl.pallas_call(
        functools.partial(kernel, dims),
        out_shape=jax.ShapeDtypeStruct((1,) + strip, jnp.bfloat16),
        in_specs=[
            pl.BlockSpec(memory_space=pl.ANY),
            pl.BlockSpec(memory_space=pltpu.SMEM),
            pl.BlockSpec(memory_space=pl.ANY),
            pl.BlockSpec(memory_space=pltpu.SMEM),
            pl.BlockSpec(memory_space=pltpu.SMEM),
        ],
        out_specs=pl.BlockSpec(memory_space=pltpu.VMEM),
        scratch_shapes=[
            pltpu.VMEM((sections, rl, side, width), jnp.bfloat16),
            pltpu.VMEM((n_row, sections, rp, side, p_width), jnp.bfloat16),
            pltpu.VMEM((n_row, codes, LANES), jnp.int32),
            pltpu.VMEM((n_col, n_row, rl * side, depth), jnp.bfloat16),
            pltpu.VMEM((n_row, depth, NCC * side), jnp.bfloat16),
            pltpu.VMEM((group * side, NCC * side), jnp.float32),
            pltpu.VMEM((group, NCC, side, LANES), jnp.float32),
            pltpu.VMEM(strip, jnp.float32),
            pltpu.VMEM((n_layer - 1,) + strip, jnp.bfloat16),
            pltpu.VMEM((n_layer - 1,) + strip, jnp.bfloat16),
            dma((2,)),
            dma((n_row - 1,)), dma((n_row - 1,)),
            dma((n_row - 1,)), dma((n_row - 1,)),
            dma((n_col - 1,)), dma((n_col - 1,)),
            dma((n_layer - 1,)), dma((n_layer - 1,)),
        ],
        compiler_params=pltpu.CompilerParams(
            collective_id=0, has_side_effects=True, vmem_limit_bytes=40 * 2**20),
    )(a_blocks, a_cols, p_blocks, p_cols, c_cols)


def solution(mesh):
    dims = tuple(mesh.shape[x] for x in ("row", "col", "layer"))
    return jax.shard_map(
        functools.partial(local, dims),
        mesh=mesh,
        in_specs=(
            P("layer", None, ("row", "col"), None, None),
            P("layer", None, ("row", "col"), None),
            P("layer", None, "col", "row", None, None),
            P("layer", None, "col", "row", None),
            P("col", "row", None),
        ),
        out_specs=P("col", ("row", "layer"), None, None),
        check_vma=False,
    )
```

```python
import functools

import jax
import jax.numpy as jnp
from jax import lax
from jax.experimental import pallas as pl
from jax.experimental.pallas import tpu as pltpu
from jax.sharding import PartitionSpec as P

MESH = pl.DeviceIdType.MESH
LANES = 128
NCC = 16


def partner(me, d, n):
    out = 0
    bit = 1
    while bit < n:
        out = out + lax.rem(lax.div(me, bit) + ((d // bit) % 2), 2) * bit
        bit *= 2
    return out


def pair_codes(values, half):
    lane = lax.broadcasted_iota(jnp.int32, (1, LANES), 1)
    low = lane < half
    codes = []
    for p in range(len(values) // 2):
        codes.append(jnp.where(low, values[2 * p], values[2 * p + 1]))
        codes.append(jnp.where(low, values[2 * p + 1], values[2 * p]))
    return codes


def pair_tiles(x, half):
    tiles = []
    for p in range(x.shape[1] // LANES):
        tile = x[:, p * LANES:(p + 1) * LANES].astype(jnp.float32)
        tiles.append(tile)
        tiles.append(pltpu.roll(tile, half, axis=1))
    return tiles


def kernel(dims, a_hbm, a_cols_hbm, p_hbm, p_cols_hbm, c_cols_hbm, out_ref,
           a_cols, p_cols, c_cols, a_v, p_all, code_all, at_all, spread, t_acc, t_pick, own, c_send, c_recv,
           in_sem, ps, pr, cs, cr, as_, ar, zs, zr):
    n_row, n_col, n_layer = dims
    sections, rl, side, width = a_v.shape
    rp = p_all.shape[2]
    group = at_all.shape[0] * rl
    own_rows = c_send.shape[1]
    kc = c_cols.shape[2]
    my_row, my_col, my_layer = (lax.axis_index(x) for x in ("row", "col", "layer"))

    barrier = pltpu.get_barrier_semaphore()
    for axis, me, n in (("row", my_row, n_row), ("col", my_col, n_col), ("layer", my_layer, n_layer)):
        for d in range(1, n):
            pl.semaphore_signal(barrier, inc=1, device_id={axis: partner(me, d, n)}, device_id_type=MESH)

    load_p = pltpu.make_async_copy(p_hbm.at[0, :, 0], p_all.at[my_row], in_sem.at[0])
    load_a = pltpu.make_async_copy(a_hbm.at[0], a_v, in_sem.at[1])
    load_pc = pltpu.make_async_copy(p_cols_hbm, p_cols, in_sem.at[2])
    load_ac = pltpu.make_async_copy(a_cols_hbm, a_cols, in_sem.at[3])
    load_cc = pltpu.make_async_copy(c_cols_hbm, c_cols, in_sem.at[4])
    for load in (load_p, load_pc, load_ac, load_a, load_cc):
        load.start()

    lane = lax.broadcasted_iota(jnp.int32, (side, LANES), 1)
    low = lane < side
    second = jnp.where(low, 0, 1)

    per_row = p_cols.shape[4]
    load_pc.wait()
    for s in range(sections):
        for r in range(rp):
            codes = pair_codes([p_cols[0, s, 0, r, j] for j in range(per_row)], side)
            for v, code in enumerate(codes):
                at = (s * rp + r) * per_row + v
                code_all[my_row, at:at + 1, :] = code

    load_ac.wait()
    load_a.wait()
    for s in range(sections):
        for i in range(rl):
            codes = pair_codes([a_cols[0, s, i, k] for k in range(width // side)], side)
            codes = [jnp.broadcast_to(code, (side, LANES)) for code in codes]
            tiles = pair_tiles(a_v[s, i], side)
            for q in range(n_row * rp // 2):
                total = jnp.zeros((side, LANES), jnp.float32)
                for code, tile in zip(codes, tiles):
                    total = total + jnp.where(code == 2 * q + second, tile, 0.0)
                slot = 2 * q // rp
                start = (s * rp + 2 * q % rp) * side
                at_all[my_col, slot, i * side:(i + 1) * side, start:start + LANES] = total.astype(jnp.bfloat16)

    load_p.wait()
    load_cc.wait()
    pl.semaphore_wait(barrier, (n_row - 1) + (n_col - 1) + (n_layer - 1))

    sends = []
    p_copies, a_copies = [], []
    for d in range(1, n_row):
        to = {"row": partner(my_row, d, n_row)}
        code_copy = pltpu.make_async_remote_copy(
            code_all.at[my_row], code_all.at[my_row], cs.at[d - 1], cr.at[d - 1], device_id=to, device_id_type=MESH)
        code_copy.start()
        copy = pltpu.make_async_remote_copy(
            p_all.at[my_row], p_all.at[my_row], ps.at[d - 1], pr.at[d - 1], device_id=to, device_id_type=MESH)
        copy.start()
        p_copies.append((code_copy, copy))
        sends += [code_copy, copy]
    for d in range(1, n_col):
        copy = pltpu.make_async_remote_copy(
            at_all.at[my_col], at_all.at[my_col], as_.at[d - 1], ar.at[d - 1],
            device_id={"col": partner(my_col, d, n_col)}, device_id_type=MESH)
        copy.start()
        a_copies.append(copy)
        sends.append(copy)

    def spread_rows(slot, to):
        for s in range(sections):
            for r in range(rp):
                codes = []
                for v in range(per_row):
                    at = (s * rp + r) * per_row + v
                    codes.append(jnp.broadcast_to(code_all[slot, at:at + 1, :], (side, LANES)))
                tiles = pair_tiles(p_all[slot, s, r], side)
                for q in range(NCC // 2):
                    total = jnp.zeros((side, LANES), jnp.float32)
                    for code, tile in zip(codes, tiles):
                        total = jnp.where(code == 2 * q + second, tile, total)
                    first = (s * rp + r) * side
                    spread[to, first:first + side, q * LANES:(q + 1) * LANES] = total.astype(jnp.bfloat16)

    step_cols = 2 * LANES
    for d in range(n_row):
        slot = partner(my_row, d, n_row)
        if d > 0:
            for copy in p_copies[d - 1]:
                copy.wait_recv()
        spread_rows(slot, d)
        if d == 0:
            for copy in a_copies:
                copy.wait_recv()
        left = at_all[:, slot].reshape(group * side, sections * rp * side)
        for n in range(0, NCC * side, step_cols):
            part = jnp.dot(left, spread[d, :, n:n + step_cols], preferred_element_type=jnp.float32)
            if d > 0:
                part = part + t_acc[:, n:n + step_cols]
            if d < n_row - 1:
                t_acc[:, n:n + step_cols] = part
            else:
                for i in range(group):
                    for h in range(step_cols // LANES):
                        tile = part[i * side:(i + 1) * side, h * LANES:(h + 1) * LANES]
                        q = n // LANES + h
                        t_pick[i, q] = tile
                        t_pick[i, NCC // 2 + q] = pltpu.roll(tile, side, axis=1)

    def pick(i, u):
        c0 = c_cols[0, i, 2 * u]
        c1 = c_cols[0, i, 2 * u + 1]
        at0 = lax.rem(c0, 2) * (NCC // 2) + lax.div(c0, 2)
        at1 = (1 - lax.rem(c1, 2)) * (NCC // 2) + lax.div(c1, 2)
        return jnp.where(low, t_pick[i, at0], t_pick[i, at1])

    z_copies = []
    for d in range(n_layer - 1, 0, -1):
        dst = partner(my_layer, d, n_layer)
        for o in range(own_rows):
            for u in range(kc // 2):
                c_send[d - 1, o, :, u * LANES:(u + 1) * LANES] = pick(dst * own_rows + o, u).astype(jnp.bfloat16)
        copy = pltpu.make_async_remote_copy(
            c_send.at[d - 1], c_recv.at[d - 1], zs.at[d - 1], zr.at[d - 1],
            device_id={"layer": dst}, device_id_type=MESH)
        copy.start()
        z_copies.append(copy)
        sends.append(copy)
    for o in range(own_rows):
        for u in range(kc // 2):
            own[o, :, u * LANES:(u + 1) * LANES] = pick(my_layer * own_rows + o, u)
    for copy in reversed(z_copies):
        copy.wait_recv()
    total = own[...]
    for d in range(1, n_layer):
        total = total + c_recv[d - 1].astype(jnp.float32)
    out_ref[0] = total.astype(jnp.bfloat16)
    for copy in sends:
        copy.wait_send()


def local(dims, a_blocks, a_cols, p_blocks, p_cols, c_cols):
    n_row, n_col, n_layer = dims
    sections, rl, side, width = a_blocks.shape[1:]
    rp, p_width = p_blocks.shape[3], p_blocks.shape[5]
    group, kc = c_cols.shape[1:]
    own_rows = group // n_layer
    codes = sections * rp * (p_width // side)
    strip = (own_rows, side, kc * side)
    depth = sections * rp * side
    dma = pltpu.SemaphoreType.DMA
    return pl.pallas_call(
        functools.partial(kernel, dims),
        out_shape=jax.ShapeDtypeStruct((1,) + strip, jnp.bfloat16),
        in_specs=[
            pl.BlockSpec(memory_space=pl.ANY),
            pl.BlockSpec(memory_space=pl.ANY),
            pl.BlockSpec(memory_space=pl.ANY),
            pl.BlockSpec(memory_space=pl.ANY),
            pl.BlockSpec(memory_space=pl.ANY),
        ],
        out_specs=pl.BlockSpec(memory_space=pltpu.VMEM),
        scratch_shapes=[
            pltpu.SMEM(a_cols.shape, jnp.int32),
            pltpu.SMEM(p_cols.shape, jnp.int32),
            pltpu.SMEM(c_cols.shape, jnp.int32),
            pltpu.VMEM((sections, rl, side, width), jnp.bfloat16),
            pltpu.VMEM((n_row, sections, rp, side, p_width), jnp.bfloat16),
            pltpu.VMEM((n_row, codes, LANES), jnp.int32),
            pltpu.VMEM((n_col, n_row, rl * side, depth), jnp.bfloat16),
            pltpu.VMEM((n_row, depth, NCC * side), jnp.bfloat16),
            pltpu.VMEM((group * side, NCC * side), jnp.float32),
            pltpu.VMEM((group, NCC, side, LANES), jnp.float32),
            pltpu.VMEM(strip, jnp.float32),
            pltpu.VMEM((n_layer - 1,) + strip, jnp.bfloat16),
            pltpu.VMEM((n_layer - 1,) + strip, jnp.bfloat16),
            dma((5,)),
            dma((n_row - 1,)), dma((n_row - 1,)),
            dma((n_row - 1,)), dma((n_row - 1,)),
            dma((n_col - 1,)), dma((n_col - 1,)),
            dma((n_layer - 1,)), dma((n_layer - 1,)),
        ],
        compiler_params=pltpu.CompilerParams(
            collective_id=0, has_side_effects=True, vmem_limit_bytes=63 * 2**20),
    )(a_blocks, a_cols, p_blocks, p_cols, c_cols)


def solution(mesh):
    dims = tuple(mesh.shape[x] for x in ("row", "col", "layer"))
    return jax.shard_map(
        functools.partial(local, dims),
        mesh=mesh,
        in_specs=(
            P("layer", None, ("row", "col"), None, None),
            P("layer", None, ("row", "col"), None),
            P("layer", None, "col", "row", None, None),
            P("layer", None, "col", "row", None),
            P("col", "row", None),
        ),
        out_specs=P("col", ("row", "layer"), None, None),
        check_vma=False,
    )
```

```python
import functools

import jax
import jax.numpy as jnp
from jax import lax
from jax.experimental import pallas as pl
from jax.experimental.pallas import tpu as pltpu
from jax.sharding import PartitionSpec as P

MESH = pl.DeviceIdType.MESH
LANES = 128
NCC = 16


def partner(me, d, n):
    out = 0
    bit = 1
    while bit < n:
        out = out + lax.rem(lax.div(me, bit) + ((d // bit) % 2), 2) * bit
        bit *= 2
    return out


def pair_codes(values, half):
    lane = lax.broadcasted_iota(jnp.int32, (1, LANES), 1)
    low = lane < half
    codes = []
    for p in range(len(values) // 2):
        codes.append(jnp.where(low, values[2 * p], values[2 * p + 1]))
        codes.append(jnp.where(low, values[2 * p + 1], values[2 * p]))
    return codes


def pair_tiles(x, half):
    tiles = []
    for p in range(x.shape[1] // LANES):
        tile = x[:, p * LANES:(p + 1) * LANES].astype(jnp.float32)
        tiles.append(tile)
        tiles.append(pltpu.roll(tile, half, axis=1))
    return tiles


def select4(lane, q, parts):
    out = parts[3]
    for g in (2, 1, 0):
        out = jnp.where(lane < (g + 1) * q, parts[g], out)
    return out


ORDER = (0, 2, 1, 3)


def pack(t0, t1, even, q):
    return jnp.where(even, t0, pltpu.roll(t1, q, axis=1)), jnp.where(even, pltpu.roll(t0, LANES - q, axis=1), t1)


def kernel(dims, a_hbm, a_cols_hbm, p_hbm, p_cols_hbm, c_cols_hbm, out_ref,
           a_cols, p_cols, c_cols, a_v, p_v, p_all, code_all, at_all, spread, t_acc, t_pick, own, c_send, c_recv,
           in_sem, ps, pr, cs, cr, as_, ar, zs, zr):
    n_row, n_col, n_layer = dims
    sections, rl, side, width = a_v.shape
    rp = p_all.shape[3]
    group = at_all.shape[0] * rl
    own_rows = c_send.shape[2]
    kc = c_cols.shape[2]
    quarter = side // 2
    tiles_t = NCC * quarter // LANES
    my_row, my_col, my_layer = (lax.axis_index(x) for x in ("row", "col", "layer"))

    barrier = pltpu.get_barrier_semaphore()
    for axis, me, n in (("row", my_row, n_row), ("col", my_col, n_col), ("layer", my_layer, n_layer)):
        for d in range(1, n):
            pl.semaphore_signal(barrier, inc=1, device_id={axis: partner(me, d, n)}, device_id_type=MESH)

    load_p = pltpu.make_async_copy(p_hbm.at[0, :, 0], p_v, in_sem.at[0])
    load_a = pltpu.make_async_copy(a_hbm.at[0], a_v, in_sem.at[1])
    load_pc = pltpu.make_async_copy(p_cols_hbm, p_cols, in_sem.at[2])
    load_ac = pltpu.make_async_copy(a_cols_hbm, a_cols, in_sem.at[3])
    load_cc = pltpu.make_async_copy(c_cols_hbm, c_cols, in_sem.at[4])
    for load in (load_p, load_pc, load_a, load_ac, load_cc):
        load.start()

    lane = lax.broadcasted_iota(jnp.int32, (side, LANES), 1)
    lane1 = lax.broadcasted_iota(jnp.int32, (1, LANES), 1)
    even = lax.rem(lax.div(lane, quarter), 2) == 0
    second = jnp.where(lane < side, 0, 1)
    fourth = lax.div(lane, quarter)

    load_pc.wait()
    for s in range(sections):
        for r in range(rp):
            cols = [p_cols[0, s, 0, r, j] for j in range(4)]
            for k in range(4):
                code = select4(lane1, quarter, [cols[ORDER[(g - k) % 4]] for g in range(4)])
                at = (s * rp + r) * 4 + k
                code_all[my_row, at:at + 1, :] = code
    load_p.wait()
    for s in range(sections):
        for r in range(rp):
            x = p_v[s, r].astype(jnp.float32)
            halves = pack(x[:, :LANES], x[:, LANES:], even, quarter)
            for h in range(2):
                p_all[h, my_row, s, r] = halves[h].astype(jnp.bfloat16)

    load_cc.wait()
    pl.semaphore_wait(barrier, (n_row - 1) + (n_col - 1) + (n_layer - 1))

    sends = []
    p_copies = [[], []]
    code_copies = []
    for d in range(1, n_row):
        to = {"row": partner(my_row, d, n_row)}
        code_copies.append(pltpu.make_async_remote_copy(
            code_all.at[my_row], code_all.at[my_row], cs.at[d - 1], cr.at[d - 1], device_id=to, device_id_type=MESH))
        for h in range(2):
            p_copies[h].append(pltpu.make_async_remote_copy(
                p_all.at[h, my_row], p_all.at[h, my_row], ps.at[h, d - 1], pr.at[h, d - 1],
                device_id=to, device_id_type=MESH))
    for copy in code_copies + p_copies[0]:
        copy.start()
    sends += code_copies

    load_ac.wait()
    load_a.wait()
    for s in range(sections):
        for i in range(rl):
            codes = pair_codes([a_cols[0, s, i, k] for k in range(width // side)], side)
            codes = [jnp.broadcast_to(code, (side, LANES)) for code in codes]
            tiles = pair_tiles(a_v[s, i], side)
            for q in range(n_row * rp // 2):
                total = jnp.zeros((side, LANES), jnp.float32)
                for code, tile in zip(codes, tiles):
                    total = total + jnp.where(code == 2 * q + second, tile, 0.0)
                slot = 2 * q // rp
                start = (s * rp + 2 * q % rp) * side
                at_all[my_col, slot, i * side:(i + 1) * side, start:start + LANES] = total.astype(jnp.bfloat16)
    a_copies = []
    for d in range(1, n_col):
        copy = pltpu.make_async_remote_copy(
            at_all.at[my_col], at_all.at[my_col], as_.at[d - 1], ar.at[d - 1],
            device_id={"col": partner(my_col, d, n_col)}, device_id_type=MESH)
        copy.start()
        a_copies.append(copy)
        sends.append(copy)

    def spread_rows(h, slot, to):
        for s in range(sections):
            for r in range(rp):
                tile = p_all[h, slot, s, r].astype(jnp.float32)
                tiles = [tile] + [pltpu.roll(tile, k * quarter, axis=1) for k in range(1, 4)]
                codes = []
                for k in range(4):
                    at = (s * rp + r) * 4 + k
                    codes.append(jnp.broadcast_to(code_all[slot, at:at + 1, :], (side, LANES)))
                for q in range(tiles_t):
                    total = jnp.zeros((side, LANES), jnp.float32)
                    for code, turned in zip(codes, tiles):
                        total = jnp.where(code == 4 * q + fourth, turned, total)
                    first = (s * rp + r) * side
                    spread[h, to, first:first + side, q * LANES:(q + 1) * LANES] = total.astype(jnp.bfloat16)

    step_cols = 2 * LANES

    def multiply(h, d):
        left = at_all[:, partner(my_row, d, n_row)].reshape(group * side, sections * rp * side)
        for n in range(0, NCC * quarter, step_cols):
            part = jnp.dot(left, spread[h, d, :, n:n + step_cols], preferred_element_type=jnp.float32)
            if d > 0:
                part = part + t_acc[h, :, n:n + step_cols]
            if d < n_row - 1:
                t_acc[h, :, n:n + step_cols] = part
                continue
            for i in range(group):
                for e in range(step_cols // LANES):
                    tile = part[i * side:(i + 1) * side, e * LANES:(e + 1) * LANES]
                    q = n // LANES + e
                    t_pick[h, i, q] = tile
                    for k in range(1, 4):
                        t_pick[h, i, k * tiles_t + q] = pltpu.roll(tile, k * quarter, axis=1)

    def pick(h, i, u):
        parts = []
        for g in range(4):
            c = c_cols[0, i, 4 * u + ORDER[g]]
            turn = lax.rem(g + 4 - lax.rem(c, 4), 4)
            parts.append(t_pick[h, i, turn * tiles_t + lax.div(c, 4)])
        return select4(lane, quarter, parts)

    for h in range(2):
        spread_rows(h, my_row, 0)
    for copy in p_copies[0]:
        copy.wait_send()
    for copy in p_copies[1]:
        copy.start()
    sends += p_copies[1]
    for copy in a_copies:
        copy.wait_recv()
    for h in range(2):
        multiply(h, 0)

    z_copies = [[], []]
    for h in range(2):
        for d in range(1, n_row):
            if h == 0:
                code_copies[d - 1].wait_recv()
            p_copies[h][d - 1].wait_recv()
            spread_rows(h, partner(my_row, d, n_row), d)
            multiply(h, d)
        for d in range(n_layer - 1, 0, -1):
            dst = partner(my_layer, d, n_layer)
            for o in range(own_rows):
                for u in range(kc // 4):
                    c_send[h, d - 1, o, :, u * LANES:(u + 1) * LANES] = pick(
                        h, dst * own_rows + o, u).astype(jnp.bfloat16)
            copy = pltpu.make_async_remote_copy(
                c_send.at[h, d - 1], c_recv.at[h, d - 1], zs.at[h, d - 1], zr.at[h, d - 1],
                device_id={"layer": dst}, device_id_type=MESH)
            copy.start()
            z_copies[h].append(copy)
            sends.append(copy)
        for o in range(own_rows):
            for u in range(kc // 4):
                own[h, o, :, u * LANES:(u + 1) * LANES] = pick(h, my_layer * own_rows + o, u)

    for h in range(2):
        for copy in z_copies[h]:
            copy.wait_recv()
        total = own[h]
        for d in range(1, n_layer):
            total = total + c_recv[h, d - 1].astype(jnp.float32)
        own[h] = total
    for o in range(own_rows):
        for u in range(kc // 4):
            h0 = own[0, o, :, u * LANES:(u + 1) * LANES]
            h1 = own[1, o, :, u * LANES:(u + 1) * LANES]
            for e, tile in enumerate(pack(h0, h1, even, quarter)):
                at = (2 * u + e) * LANES
                out_ref[0, o, :, at:at + LANES] = tile.astype(jnp.bfloat16)
    for copy in sends:
        copy.wait_send()


def local(dims, a_blocks, a_cols, p_blocks, p_cols, c_cols):
    n_row, n_col, n_layer = dims
    sections, rl, side, width = a_blocks.shape[1:]
    rp, p_width = p_blocks.shape[3], p_blocks.shape[5]
    group, kc = c_cols.shape[1:]
    own_rows = group // n_layer
    strip = (own_rows, side, kc * side)
    half_strip = (own_rows, side, kc * side // 2)
    depth = sections * rp * side
    dma = pltpu.SemaphoreType.DMA
    return pl.pallas_call(
        functools.partial(kernel, dims),
        out_shape=jax.ShapeDtypeStruct((1,) + strip, jnp.bfloat16),
        in_specs=[pl.BlockSpec(memory_space=pl.ANY)] * 5,
        out_specs=pl.BlockSpec(memory_space=pltpu.VMEM),
        scratch_shapes=[
            pltpu.SMEM(a_cols.shape, jnp.int32),
            pltpu.SMEM(p_cols.shape, jnp.int32),
            pltpu.SMEM(c_cols.shape, jnp.int32),
            pltpu.VMEM((sections, rl, side, width), jnp.bfloat16),
            pltpu.VMEM((sections, rp, side, p_width), jnp.bfloat16),
            pltpu.VMEM((2, n_row, sections, rp, side, LANES), jnp.bfloat16),
            pltpu.VMEM((n_row, sections * rp * 4, LANES), jnp.int32),
            pltpu.VMEM((n_col, n_row, rl * side, depth), jnp.bfloat16),
            pltpu.VMEM((2, n_row, depth, NCC * side // 2), jnp.bfloat16),
            pltpu.VMEM((2, group * side, NCC * side // 2), jnp.float32),
            pltpu.VMEM((2, group, NCC, side, LANES), jnp.float32),
            pltpu.VMEM((2,) + half_strip, jnp.float32),
            pltpu.VMEM((2, n_layer - 1) + half_strip, jnp.bfloat16),
            pltpu.VMEM((2, n_layer - 1) + half_strip, jnp.bfloat16),
            dma((5,)),
            dma((2, n_row - 1)), dma((2, n_row - 1)),
            dma((n_row - 1,)), dma((n_row - 1,)),
            dma((n_col - 1,)), dma((n_col - 1,)),
            dma((2, n_layer - 1)), dma((2, n_layer - 1)),
        ],
        compiler_params=pltpu.CompilerParams(
            collective_id=0, has_side_effects=True, vmem_limit_bytes=63 * 2**20),
    )(a_blocks, a_cols, p_blocks, p_cols, c_cols)


def solution(mesh):
    dims = tuple(mesh.shape[x] for x in ("row", "col", "layer"))
    return jax.shard_map(
        functools.partial(local, dims),
        mesh=mesh,
        in_specs=(
            P("layer", None, ("row", "col"), None, None),
            P("layer", None, ("row", "col"), None),
            P("layer", None, "col", "row", None, None),
            P("layer", None, "col", "row", None),
            P("col", "row", None),
        ),
        out_specs=P("col", ("row", "layer"), None, None),
        check_vma=False,
    )
```

```python
import functools

import jax
import jax.numpy as jnp
from jax import lax
from jax.experimental import pallas as pl
from jax.experimental.pallas import tpu as pltpu
from jax.sharding import PartitionSpec as P

MESH = pl.DeviceIdType.MESH
LANES = 128
NCC = 16


def partner(me, d, n):
    out = 0
    bit = 1
    while bit < n:
        out = out + lax.rem(lax.div(me, bit) + ((d // bit) % 2), 2) * bit
        bit *= 2
    return out


def pair_codes(values, half):
    lane = lax.broadcasted_iota(jnp.int32, (1, LANES), 1)
    low = lane < half
    codes = []
    for p in range(len(values) // 2):
        codes.append(jnp.where(low, values[2 * p], values[2 * p + 1]))
        codes.append(jnp.where(low, values[2 * p + 1], values[2 * p]))
    return codes


def pair_tiles(x, half):
    tiles = []
    for p in range(x.shape[1] // LANES):
        tile = x[:, p * LANES:(p + 1) * LANES].astype(jnp.float32)
        tiles.append(tile)
        tiles.append(pltpu.roll(tile, half, axis=1))
    return tiles


def select4(lane, q, parts):
    out = parts[3]
    for g in (2, 1, 0):
        out = jnp.where(lane < (g + 1) * q, parts[g], out)
    return out


ORDER = (0, 2, 1, 3)


def pack(t0, t1, even, q):
    return jnp.where(even, t0, pltpu.roll(t1, q, axis=1)), jnp.where(even, pltpu.roll(t0, LANES - q, axis=1), t1)


def kernel(dims, a_hbm, a_cols_hbm, p_hbm, p_cols_hbm, c_cols_hbm, out_ref,
           a_cols, p_cols, c_cols, a_v, p_v, p_all, code_all, at_all, spread, t_acc, t_pick, own, c_send, c_recv,
           in_sem, ps, pr, cs, cr, as_, ar, zs, zr):
    n_row, n_col, n_layer = dims
    sections, rl, side, width = a_v.shape
    rp = p_all.shape[3]
    group = at_all.shape[0] * rl
    own_rows = c_send.shape[2]
    kc = c_cols.shape[2]
    quarter = side // 2
    tiles_t = NCC * quarter // LANES
    my_row, my_col, my_layer = (lax.axis_index(x) for x in ("row", "col", "layer"))

    barrier = pltpu.get_barrier_semaphore()
    for axis, me, n in (("row", my_row, n_row), ("col", my_col, n_col), ("layer", my_layer, n_layer)):
        for d in range(1, n):
            pl.semaphore_signal(barrier, inc=1, device_id={axis: partner(me, d, n)}, device_id_type=MESH)

    load_p = pltpu.make_async_copy(p_hbm.at[0, :, 0], p_v, in_sem.at[0])
    load_a = pltpu.make_async_copy(a_hbm.at[0], a_v, in_sem.at[1])
    load_pc = pltpu.make_async_copy(p_cols_hbm, p_cols, in_sem.at[2])
    load_ac = pltpu.make_async_copy(a_cols_hbm, a_cols, in_sem.at[3])
    load_cc = pltpu.make_async_copy(c_cols_hbm, c_cols, in_sem.at[4])
    for load in (load_p, load_pc, load_a, load_ac, load_cc):
        load.start()

    lane = lax.broadcasted_iota(jnp.int32, (side, LANES), 1)
    lane1 = lax.broadcasted_iota(jnp.int32, (1, LANES), 1)
    even = lax.rem(lax.div(lane, quarter), 2) == 0
    second = jnp.where(lane < side, 0, 1)
    fourth = lax.div(lane, quarter)

    load_pc.wait()
    for s in range(sections):
        for r in range(rp):
            cols = [p_cols[0, s, 0, r, j] for j in range(4)]
            for k in range(4):
                code = select4(lane1, quarter, [cols[ORDER[(g - k) % 4]] for g in range(4)])
                at = (s * rp + r) * 4 + k
                code_all[my_row, at:at + 1, :] = code
    load_p.wait()
    for s in range(sections):
        for r in range(rp):
            x = p_v[s, r].astype(jnp.float32)
            halves = pack(x[:, :LANES], x[:, LANES:], even, quarter)
            for h in range(2):
                p_all[h, my_row, s, r] = halves[h].astype(jnp.bfloat16)

    load_cc.wait()
    pl.semaphore_wait(barrier, (n_row - 1) + (n_col - 1) + (n_layer - 1))

    sends = []
    p_copies = [[], []]
    code_copies = []
    for d in range(1, n_row):
        to = {"row": partner(my_row, d, n_row)}
        code_copies.append(pltpu.make_async_remote_copy(
            code_all.at[my_row], code_all.at[my_row], cs.at[d - 1], cr.at[d - 1], device_id=to, device_id_type=MESH))
        for h in range(2):
            p_copies[h].append(pltpu.make_async_remote_copy(
                p_all.at[h, my_row], p_all.at[h, my_row], ps.at[h, d - 1], pr.at[h, d - 1],
                device_id=to, device_id_type=MESH))
    early = list(range(n_row - 2))
    last = n_row - 2
    for d in early:
        code_copies[d].start()
        p_copies[0][d].start()
    code_copies[last].start()
    sends += code_copies

    load_ac.wait()
    load_a.wait()
    for s in range(sections):
        for i in range(rl):
            codes = pair_codes([a_cols[0, s, i, k] for k in range(width // side)], side)
            codes = [jnp.broadcast_to(code, (side, LANES)) for code in codes]
            tiles = pair_tiles(a_v[s, i], side)
            for q in range(n_row * rp // 2):
                total = jnp.zeros((side, LANES), jnp.float32)
                for code, tile in zip(codes, tiles):
                    total = total + jnp.where(code == 2 * q + second, tile, 0.0)
                slot = 2 * q // rp
                start = (s * rp + 2 * q % rp) * side
                at_all[my_col, slot, i * side:(i + 1) * side, start:start + LANES] = total.astype(jnp.bfloat16)
    a_copies = []
    for d in range(1, n_col):
        copy = pltpu.make_async_remote_copy(
            at_all.at[my_col], at_all.at[my_col], as_.at[d - 1], ar.at[d - 1],
            device_id={"col": partner(my_col, d, n_col)}, device_id_type=MESH)
        copy.start()
        a_copies.append(copy)
        sends.append(copy)

    def spread_rows(h, slot, to):
        for s in range(sections):
            for r in range(rp):
                tile = p_all[h, slot, s, r].astype(jnp.float32)
                tiles = [tile] + [pltpu.roll(tile, k * quarter, axis=1) for k in range(1, 4)]
                codes = []
                for k in range(4):
                    at = (s * rp + r) * 4 + k
                    codes.append(jnp.broadcast_to(code_all[slot, at:at + 1, :], (side, LANES)))
                for q in range(tiles_t):
                    total = jnp.zeros((side, LANES), jnp.float32)
                    for code, turned in zip(codes, tiles):
                        total = jnp.where(code == 4 * q + fourth, turned, total)
                    first = (s * rp + r) * side
                    spread[h, to, first:first + side, q * LANES:(q + 1) * LANES] = total.astype(jnp.bfloat16)

    step_cols = 2 * LANES

    def multiply(h, d):
        left = at_all[:, partner(my_row, d, n_row)].reshape(group * side, sections * rp * side)
        for n in range(0, NCC * quarter, step_cols):
            part = jnp.dot(left, spread[h, d, :, n:n + step_cols], preferred_element_type=jnp.float32)
            part = part.reshape(group, side, step_cols)
            if d > 0:
                part = part + t_acc[h, :, :, n:n + step_cols]
            t_acc[h, :, :, n:n + step_cols] = part

    def turn_row(h, i):
        for q in range(tiles_t):
            tile = t_acc[h, i, :, q * LANES:(q + 1) * LANES]
            t_pick[h, i, q] = tile
            for k in range(1, 4):
                t_pick[h, i, k * tiles_t + q] = pltpu.roll(tile, k * quarter, axis=1)

    def pick(h, i, u):
        parts = []
        for g in range(4):
            c = c_cols[0, i, 4 * u + ORDER[g]]
            turn = lax.rem(g + 4 - lax.rem(c, 4), 4)
            parts.append(t_pick[h, i, turn * tiles_t + lax.div(c, 4)])
        return select4(lane, quarter, parts)

    def leave(h, which):
        for d in which:
            p_copies[h][d].wait_send()

    def receive(h, d):
        if h == 0:
            code_copies[d - 1].wait_recv()
        p_copies[h][d - 1].wait_recv()
        spread_rows(h, partner(my_row, d, n_row), d)
        multiply(h, d)

    spread_rows(0, my_row, 0)
    leave(0, early)
    p_copies[0][last].start()
    spread_rows(1, my_row, 0)
    for copy in a_copies:
        copy.wait_recv()
    for h in range(2):
        multiply(h, 0)

    z_copies = [[], []]
    for h in range(2):
        for d in range(1, n_row - 1):
            receive(h, d)
        if h == 0:
            leave(0, [last])
            for d in early:
                p_copies[1][d].start()
        receive(h, n_row - 1)
        if h == 0:
            leave(1, early)
            p_copies[1][last].start()
            sends.append(p_copies[1][last])
        for d in range(n_layer - 1, 0, -1):
            dst = partner(my_layer, d, n_layer)
            for o in range(own_rows):
                turn_row(h, dst * own_rows + o)
                for u in range(kc // 4):
                    c_send[h, d - 1, o, :, u * LANES:(u + 1) * LANES] = pick(
                        h, dst * own_rows + o, u).astype(jnp.bfloat16)
            copy = pltpu.make_async_remote_copy(
                c_send.at[h, d - 1], c_recv.at[h, d - 1], zs.at[h, d - 1], zr.at[h, d - 1],
                device_id={"layer": dst}, device_id_type=MESH)
            copy.start()
            z_copies[h].append(copy)
            sends.append(copy)
        for o in range(own_rows):
            turn_row(h, my_layer * own_rows + o)
            for u in range(kc // 4):
                own[h, o, :, u * LANES:(u + 1) * LANES] = pick(h, my_layer * own_rows + o, u)

    for h in range(2):
        for copy in z_copies[h]:
            copy.wait_recv()
        total = own[h]
        for d in range(1, n_layer):
            total = total + c_recv[h, d - 1].astype(jnp.float32)
        own[h] = total
    for o in range(own_rows):
        for u in range(kc // 4):
            h0 = own[0, o, :, u * LANES:(u + 1) * LANES]
            h1 = own[1, o, :, u * LANES:(u + 1) * LANES]
            for e, tile in enumerate(pack(h0, h1, even, quarter)):
                at = (2 * u + e) * LANES
                out_ref[0, o, :, at:at + LANES] = tile.astype(jnp.bfloat16)
    for copy in sends:
        copy.wait_send()


def local(dims, a_blocks, a_cols, p_blocks, p_cols, c_cols):
    n_row, n_col, n_layer = dims
    sections, rl, side, width = a_blocks.shape[1:]
    rp, p_width = p_blocks.shape[3], p_blocks.shape[5]
    group, kc = c_cols.shape[1:]
    own_rows = group // n_layer
    strip = (own_rows, side, kc * side)
    half_strip = (own_rows, side, kc * side // 2)
    depth = sections * rp * side
    dma = pltpu.SemaphoreType.DMA
    return pl.pallas_call(
        functools.partial(kernel, dims),
        out_shape=jax.ShapeDtypeStruct((1,) + strip, jnp.bfloat16),
        in_specs=[pl.BlockSpec(memory_space=pl.ANY)] * 5,
        out_specs=pl.BlockSpec(memory_space=pltpu.VMEM),
        scratch_shapes=[
            pltpu.SMEM(a_cols.shape, jnp.int32),
            pltpu.SMEM(p_cols.shape, jnp.int32),
            pltpu.SMEM(c_cols.shape, jnp.int32),
            pltpu.VMEM((sections, rl, side, width), jnp.bfloat16),
            pltpu.VMEM((sections, rp, side, p_width), jnp.bfloat16),
            pltpu.VMEM((2, n_row, sections, rp, side, LANES), jnp.bfloat16),
            pltpu.VMEM((n_row, sections * rp * 4, LANES), jnp.int32),
            pltpu.VMEM((n_col, n_row, rl * side, depth), jnp.bfloat16),
            pltpu.VMEM((2, n_row, depth, NCC * side // 2), jnp.bfloat16),
            pltpu.VMEM((2, group, side, NCC * side // 2), jnp.float32),
            pltpu.VMEM((2, group, NCC, side, LANES), jnp.float32),
            pltpu.VMEM((2,) + half_strip, jnp.float32),
            pltpu.VMEM((2, n_layer - 1) + half_strip, jnp.bfloat16),
            pltpu.VMEM((2, n_layer - 1) + half_strip, jnp.bfloat16),
            dma((5,)),
            dma((2, n_row - 1)), dma((2, n_row - 1)),
            dma((n_row - 1,)), dma((n_row - 1,)),
            dma((n_col - 1,)), dma((n_col - 1,)),
            dma((2, n_layer - 1)), dma((2, n_layer - 1)),
        ],
        compiler_params=pltpu.CompilerParams(
            collective_id=0, has_side_effects=True, vmem_limit_bytes=63 * 2**20),
    )(a_blocks, a_cols, p_blocks, p_cols, c_cols)


def solution(mesh):
    dims = tuple(mesh.shape[x] for x in ("row", "col", "layer"))
    return jax.shard_map(
        functools.partial(local, dims),
        mesh=mesh,
        in_specs=(
            P("layer", None, ("row", "col"), None, None),
            P("layer", None, ("row", "col"), None),
            P("layer", None, "col", "row", None, None),
            P("layer", None, "col", "row", None),
            P("col", "row", None),
        ),
        out_specs=P("col", ("row", "layer"), None, None),
        check_vma=False,
    )
```

```python
import functools

import jax
import jax.numpy as jnp
from jax import lax
from jax.experimental import pallas as pl
from jax.experimental.pallas import tpu as pltpu
from jax.sharding import PartitionSpec as P

MESH = pl.DeviceIdType.MESH
LANES = 128
NCC = 16


def partner(me, d, n):
    out = 0
    bit = 1
    while bit < n:
        out = out + lax.rem(lax.div(me, bit) + ((d // bit) % 2), 2) * bit
        bit *= 2
    return out


def pair_codes(values, half):
    lane = lax.broadcasted_iota(jnp.int32, (1, LANES), 1)
    low = lane < half
    codes = []
    for p in range(len(values) // 2):
        codes.append(jnp.where(low, values[2 * p], values[2 * p + 1]))
        codes.append(jnp.where(low, values[2 * p + 1], values[2 * p]))
    return codes


def pair_tiles(x, half):
    tiles = []
    for p in range(x.shape[1] // LANES):
        tile = x[:, p * LANES:(p + 1) * LANES].astype(jnp.float32)
        tiles.append(tile)
        tiles.append(pltpu.roll(tile, half, axis=1))
    return tiles


def select4(lane, q, parts):
    out = parts[3]
    for g in (2, 1, 0):
        out = jnp.where(lane < (g + 1) * q, parts[g], out)
    return out


ORDER = (0, 2, 1, 3)


def pack(t0, t1, even, q):
    return jnp.where(even, t0, pltpu.roll(t1, q, axis=1)), jnp.where(even, pltpu.roll(t0, LANES - q, axis=1), t1)


def kernel(dims, a_hbm, a_cols_hbm, p_hbm, p_cols_hbm, c_cols_hbm, out_ref,
           a_cols, p_cols, c_cols, a_v, p_v, p_all, code_all, at_all, spread, t_acc, t_pick, own, c_send, c_recv,
           in_sem, ps, pr, cs, cr, as_, ar, zs, zr):
    n_row, n_col, n_layer = dims
    sections, rl, side, width = a_v.shape
    rp = p_all.shape[3]
    group = at_all.shape[0] * rl
    own_rows = c_send.shape[2]
    kc = c_cols.shape[2]
    quarter = side // 2
    tiles_t = NCC * quarter // LANES
    my_row, my_col, my_layer = (lax.axis_index(x) for x in ("row", "col", "layer"))

    barrier = pltpu.get_barrier_semaphore()
    for axis, me, n in (("row", my_row, n_row), ("col", my_col, n_col), ("layer", my_layer, n_layer)):
        for d in range(1, n):
            pl.semaphore_signal(barrier, inc=1, device_id={axis: partner(me, d, n)}, device_id_type=MESH)

    load_p = pltpu.make_async_copy(p_hbm.at[0, :, 0], p_v, in_sem.at[0])
    load_a = pltpu.make_async_copy(a_hbm.at[0], a_v, in_sem.at[1])
    load_pc = pltpu.make_async_copy(p_cols_hbm, p_cols, in_sem.at[2])
    load_ac = pltpu.make_async_copy(a_cols_hbm, a_cols, in_sem.at[3])
    load_cc = pltpu.make_async_copy(c_cols_hbm, c_cols, in_sem.at[4])
    for load in (load_p, load_pc, load_a, load_ac, load_cc):
        load.start()

    lane = lax.broadcasted_iota(jnp.int32, (side, LANES), 1)
    lane1 = lax.broadcasted_iota(jnp.int32, (1, LANES), 1)
    even = lax.rem(lax.div(lane, quarter), 2) == 0
    second = jnp.where(lane < side, 0, 1)
    fourth = lax.div(lane, quarter)

    load_pc.wait()
    for s in range(sections):
        for r in range(rp):
            cols = [p_cols[0, s, 0, r, j] for j in range(4)]
            for k in range(4):
                code = select4(lane1, quarter, [cols[ORDER[(g - k) % 4]] for g in range(4)])
                at = (s * rp + r) * 4 + k
                code_all[my_row, at:at + 1, :] = code
    load_p.wait()
    for s in range(sections):
        for r in range(rp):
            x = p_v[s, r].astype(jnp.float32)
            halves = pack(x[:, :LANES], x[:, LANES:], even, quarter)
            for h in range(2):
                p_all[h, my_row, s, r] = halves[h].astype(jnp.bfloat16)

    load_cc.wait()
    pl.semaphore_wait(barrier, (n_row - 1) + (n_col - 1) + (n_layer - 1))

    sends = []
    p_copies = [[], []]
    code_copies = []
    for d in range(1, n_row):
        to = {"row": partner(my_row, d, n_row)}
        code_copies.append(pltpu.make_async_remote_copy(
            code_all.at[my_row], code_all.at[my_row], cs.at[d - 1], cr.at[d - 1], device_id=to, device_id_type=MESH))
        for h in range(2):
            p_copies[h].append(pltpu.make_async_remote_copy(
                p_all.at[h, my_row], p_all.at[h, my_row], ps.at[h, d - 1], pr.at[h, d - 1],
                device_id=to, device_id_type=MESH))
    for copy in code_copies + p_copies[0] + p_copies[1]:
        copy.start()
        sends.append(copy)

    load_ac.wait()
    load_a.wait()
    for s in range(sections):
        for i in range(rl):
            codes = pair_codes([a_cols[0, s, i, k] for k in range(width // side)], side)
            codes = [jnp.broadcast_to(code, (side, LANES)) for code in codes]
            tiles = pair_tiles(a_v[s, i], side)
            for q in range(n_row * rp // 2):
                total = jnp.zeros((side, LANES), jnp.float32)
                for code, tile in zip(codes, tiles):
                    total = total + jnp.where(code == 2 * q + second, tile, 0.0)
                slot = 2 * q // rp
                start = (s * rp + 2 * q % rp) * side
                at_all[my_col, slot, i * side:(i + 1) * side, start:start + LANES] = total.astype(jnp.bfloat16)
    a_copies = []
    for d in range(1, n_col):
        copy = pltpu.make_async_remote_copy(
            at_all.at[my_col], at_all.at[my_col], as_.at[d - 1], ar.at[d - 1],
            device_id={"col": partner(my_col, d, n_col)}, device_id_type=MESH)
        copy.start()
        a_copies.append(copy)
        sends.append(copy)

    def spread_rows(h, slot, to):
        for s in range(sections):
            for r in range(rp):
                tile = p_all[h, slot, s, r].astype(jnp.float32)
                tiles = [tile] + [pltpu.roll(tile, k * quarter, axis=1) for k in range(1, 4)]
                codes = []
                for k in range(4):
                    at = (s * rp + r) * 4 + k
                    codes.append(jnp.broadcast_to(code_all[slot, at:at + 1, :], (side, LANES)))
                for q in range(tiles_t):
                    total = jnp.zeros((side, LANES), jnp.float32)
                    for code, turned in zip(codes, tiles):
                        total = jnp.where(code == 4 * q + fourth, turned, total)
                    first = (s * rp + r) * side
                    spread[h, to, first:first + side, q * LANES:(q + 1) * LANES] = total.astype(jnp.bfloat16)

    step_cols = 2 * LANES

    def multiply(h, d):
        left = at_all[:, partner(my_row, d, n_row)].reshape(group * side, sections * rp * side)
        for n in range(0, NCC * quarter, step_cols):
            part = jnp.dot(left, spread[h, d, :, n:n + step_cols], preferred_element_type=jnp.float32)
            part = part.reshape(group, side, step_cols)
            if d > 0:
                part = part + t_acc[h, :, :, n:n + step_cols]
            t_acc[h, :, :, n:n + step_cols] = part

    def turn_row(h, i):
        for q in range(tiles_t):
            tile = t_acc[h, i, :, q * LANES:(q + 1) * LANES]
            t_pick[h, i, q] = tile
            for k in range(1, 4):
                t_pick[h, i, k * tiles_t + q] = pltpu.roll(tile, k * quarter, axis=1)

    def pick(h, i, u):
        parts = []
        for g in range(4):
            c = c_cols[0, i, 4 * u + ORDER[g]]
            turn = lax.rem(g + 4 - lax.rem(c, 4), 4)
            parts.append(t_pick[h, i, turn * tiles_t + lax.div(c, 4)])
        return select4(lane, quarter, parts)

    def receive(h, d):
        if h == 0:
            code_copies[d - 1].wait_recv()
        p_copies[h][d - 1].wait_recv()
        spread_rows(h, partner(my_row, d, n_row), d)
        multiply(h, d)

    for h in range(2):
        spread_rows(h, my_row, 0)
    for copy in a_copies:
        copy.wait_recv()
    for h in range(2):
        multiply(h, 0)

    z_copies = [[], []]
    for h in range(2):
        for d in range(1, n_row):
            receive(h, d)
        for d in range(n_layer - 1, 0, -1):
            dst = partner(my_layer, d, n_layer)
            for o in range(own_rows):
                turn_row(h, dst * own_rows + o)
                for u in range(kc // 4):
                    c_send[h, d - 1, o, :, u * LANES:(u + 1) * LANES] = pick(
                        h, dst * own_rows + o, u).astype(jnp.bfloat16)
            copy = pltpu.make_async_remote_copy(
                c_send.at[h, d - 1], c_recv.at[h, d - 1], zs.at[h, d - 1], zr.at[h, d - 1],
                device_id={"layer": dst}, device_id_type=MESH)
            copy.start()
            z_copies[h].append(copy)
            sends.append(copy)
        for o in range(own_rows):
            turn_row(h, my_layer * own_rows + o)
            for u in range(kc // 4):
                own[h, o, :, u * LANES:(u + 1) * LANES] = pick(h, my_layer * own_rows + o, u)

    for h in range(2):
        for copy in z_copies[h]:
            copy.wait_recv()
        total = own[h]
        for d in range(1, n_layer):
            total = total + c_recv[h, d - 1].astype(jnp.float32)
        own[h] = total
    for o in range(own_rows):
        for u in range(kc // 4):
            h0 = own[0, o, :, u * LANES:(u + 1) * LANES]
            h1 = own[1, o, :, u * LANES:(u + 1) * LANES]
            for e, tile in enumerate(pack(h0, h1, even, quarter)):
                at = (2 * u + e) * LANES
                out_ref[0, o, :, at:at + LANES] = tile.astype(jnp.bfloat16)
    for copy in sends:
        copy.wait_send()


def local(dims, a_blocks, a_cols, p_blocks, p_cols, c_cols):
    n_row, n_col, n_layer = dims
    sections, rl, side, width = a_blocks.shape[1:]
    rp, p_width = p_blocks.shape[3], p_blocks.shape[5]
    group, kc = c_cols.shape[1:]
    own_rows = group // n_layer
    strip = (own_rows, side, kc * side)
    half_strip = (own_rows, side, kc * side // 2)
    depth = sections * rp * side
    dma = pltpu.SemaphoreType.DMA
    return pl.pallas_call(
        functools.partial(kernel, dims),
        out_shape=jax.ShapeDtypeStruct((1,) + strip, jnp.bfloat16),
        in_specs=[pl.BlockSpec(memory_space=pl.ANY)] * 5,
        out_specs=pl.BlockSpec(memory_space=pltpu.VMEM),
        scratch_shapes=[
            pltpu.SMEM(a_cols.shape, jnp.int32),
            pltpu.SMEM(p_cols.shape, jnp.int32),
            pltpu.SMEM(c_cols.shape, jnp.int32),
            pltpu.VMEM((sections, rl, side, width), jnp.bfloat16),
            pltpu.VMEM((sections, rp, side, p_width), jnp.bfloat16),
            pltpu.VMEM((2, n_row, sections, rp, side, LANES), jnp.bfloat16),
            pltpu.VMEM((n_row, sections * rp * 4, LANES), jnp.int32),
            pltpu.VMEM((n_col, n_row, rl * side, depth), jnp.bfloat16),
            pltpu.VMEM((2, n_row, depth, NCC * side // 2), jnp.bfloat16),
            pltpu.VMEM((2, group, side, NCC * side // 2), jnp.float32),
            pltpu.VMEM((2, group, NCC, side, LANES), jnp.float32),
            pltpu.VMEM((2,) + half_strip, jnp.float32),
            pltpu.VMEM((2, n_layer - 1) + half_strip, jnp.bfloat16),
            pltpu.VMEM((2, n_layer - 1) + half_strip, jnp.bfloat16),
            dma((5,)),
            dma((2, n_row - 1)), dma((2, n_row - 1)),
            dma((n_row - 1,)), dma((n_row - 1,)),
            dma((n_col - 1,)), dma((n_col - 1,)),
            dma((2, n_layer - 1)), dma((2, n_layer - 1)),
        ],
        compiler_params=pltpu.CompilerParams(
            collective_id=0, has_side_effects=True, vmem_limit_bytes=63 * 2**20),
    )(a_blocks, a_cols, p_blocks, p_cols, c_cols)


def solution(mesh):
    dims = tuple(mesh.shape[x] for x in ("row", "col", "layer"))
    return jax.shard_map(
        functools.partial(local, dims),
        mesh=mesh,
        in_specs=(
            P("layer", None, ("row", "col"), None, None),
            P("layer", None, ("row", "col"), None),
            P("layer", None, "col", "row", None, None),
            P("layer", None, "col", "row", None),
            P("col", "row", None),
        ),
        out_specs=P("col", ("row", "layer"), None, None),
        check_vma=False,
    )
```

```python
import functools

import jax
import jax.numpy as jnp
from jax import lax
from jax.experimental import pallas as pl
from jax.experimental.pallas import tpu as pltpu
from jax.sharding import PartitionSpec as P

MESH = pl.DeviceIdType.MESH
LANES = 128
NCC = 16


def partner(me, d, n):
    out = 0
    bit = 1
    while bit < n:
        out = out + lax.rem(lax.div(me, bit) + ((d // bit) % 2), 2) * bit
        bit *= 2
    return out


def pair_codes(values, half):
    lane = lax.broadcasted_iota(jnp.int32, (1, LANES), 1)
    low = lane < half
    codes = []
    for p in range(len(values) // 2):
        codes.append(jnp.where(low, values[2 * p], values[2 * p + 1]))
        codes.append(jnp.where(low, values[2 * p + 1], values[2 * p]))
    return codes


def pair_tiles(x, half):
    tiles = []
    for p in range(x.shape[1] // LANES):
        tile = x[:, p * LANES:(p + 1) * LANES].astype(jnp.float32)
        tiles.append(tile)
        tiles.append(pltpu.roll(tile, half, axis=1))
    return tiles


def select4(lane, q, parts):
    out = parts[3]
    for g in (2, 1, 0):
        out = jnp.where(lane < (g + 1) * q, parts[g], out)
    return out


ORDER = (0, 2, 1, 3)


def pack(t0, t1, even, q):
    return jnp.where(even, t0, pltpu.roll(t1, q, axis=1)), jnp.where(even, pltpu.roll(t0, LANES - q, axis=1), t1)


def kernel(dims, a_hbm, a_cols_hbm, p_hbm, p_cols_hbm, c_cols_hbm, out_ref,
           a_cols, p_cols, c_cols, a_v, p_v, p_all, code_all, at_all, spread, t_acc, t_pick, own, c_send, c_recv, via,
           in_sem, ps, pr, cs, cr, as_, ar, zs, zr, vs, vr):
    n_row, n_col, n_layer = dims
    sections, rl, side, width = a_v.shape
    rp = p_all.shape[3]
    group = at_all.shape[0] * rl
    own_rows = c_send.shape[2]
    kc = c_cols.shape[2]
    quarter = side // 2
    tiles_t = NCC * quarter // LANES
    my_row, my_col, my_layer = (lax.axis_index(x) for x in ("row", "col", "layer"))

    barrier = pltpu.get_barrier_semaphore()
    for axis, me, n in (("row", my_row, n_row), ("col", my_col, n_col), ("layer", my_layer, n_layer)):
        for d in range(1, n):
            pl.semaphore_signal(barrier, inc=1, device_id={axis: partner(me, d, n)}, device_id_type=MESH)

    load_p = pltpu.make_async_copy(p_hbm.at[0, :, 0], p_v, in_sem.at[0])
    load_a = pltpu.make_async_copy(a_hbm.at[0], a_v, in_sem.at[1])
    load_pc = pltpu.make_async_copy(p_cols_hbm, p_cols, in_sem.at[2])
    load_ac = pltpu.make_async_copy(a_cols_hbm, a_cols, in_sem.at[3])
    load_cc = pltpu.make_async_copy(c_cols_hbm, c_cols, in_sem.at[4])
    for load in (load_p, load_pc, load_a, load_ac, load_cc):
        load.start()

    lane = lax.broadcasted_iota(jnp.int32, (side, LANES), 1)
    lane1 = lax.broadcasted_iota(jnp.int32, (1, LANES), 1)
    even = lax.rem(lax.div(lane, quarter), 2) == 0
    second = jnp.where(lane < side, 0, 1)
    fourth = lax.div(lane, quarter)

    load_pc.wait()
    for s in range(sections):
        for r in range(rp):
            cols = [p_cols[0, s, 0, r, j] for j in range(4)]
            for k in range(4):
                code = select4(lane1, quarter, [cols[ORDER[(g - k) % 4]] for g in range(4)])
                at = (s * rp + r) * 4 + k
                code_all[my_row, at:at + 1, :] = code
    load_p.wait()
    for s in range(sections):
        for r in range(rp):
            x = p_v[s, r].astype(jnp.float32)
            halves = pack(x[:, :LANES], x[:, LANES:], even, quarter)
            for h in range(2):
                p_all[h, my_row, s, r] = halves[h].astype(jnp.bfloat16)

    load_cc.wait()
    pl.semaphore_wait(barrier, (n_row - 1) + (n_col - 1) + (n_layer - 1))

    sends = []
    p_copies = [[], []]
    code_copies = []
    for d in range(1, n_row):
        to = {"row": partner(my_row, d, n_row)}
        code_copies.append(pltpu.make_async_remote_copy(
            code_all.at[my_row], code_all.at[my_row], cs.at[d - 1], cr.at[d - 1], device_id=to, device_id_type=MESH))
        for h in range(2):
            p_copies[h].append(pltpu.make_async_remote_copy(
                p_all.at[h, my_row], p_all.at[h, my_row], ps.at[h, d - 1], pr.at[h, d - 1],
                device_id=to, device_id_type=MESH))
    for copy in code_copies + p_copies[0] + p_copies[1]:
        copy.start()
        sends.append(copy)

    load_ac.wait()
    load_a.wait()
    for s in range(sections):
        for i in range(rl):
            codes = pair_codes([a_cols[0, s, i, k] for k in range(width // side)], side)
            codes = [jnp.broadcast_to(code, (side, LANES)) for code in codes]
            tiles = pair_tiles(a_v[s, i], side)
            for q in range(n_row * rp // 2):
                total = jnp.zeros((side, LANES), jnp.float32)
                for code, tile in zip(codes, tiles):
                    total = total + jnp.where(code == 2 * q + second, tile, 0.0)
                slot = 2 * q // rp
                start = (s * rp + 2 * q % rp) * side
                at_all[my_col, slot, i * side:(i + 1) * side, start:start + LANES] = total.astype(jnp.bfloat16)
    a_copies = []
    for d in range(1, n_col):
        copy = pltpu.make_async_remote_copy(
            at_all.at[my_col], at_all.at[my_col], as_.at[d - 1], ar.at[d - 1],
            device_id={"col": partner(my_col, d, n_col)}, device_id_type=MESH)
        copy.start()
        a_copies.append(copy)
        sends.append(copy)

    def spread_rows(h, slot, to):
        for s in range(sections):
            for r in range(rp):
                tile = p_all[h, slot, s, r].astype(jnp.float32)
                tiles = [tile] + [pltpu.roll(tile, k * quarter, axis=1) for k in range(1, 4)]
                codes = []
                for k in range(4):
                    at = (s * rp + r) * 4 + k
                    codes.append(jnp.broadcast_to(code_all[slot, at:at + 1, :], (side, LANES)))
                for q in range(tiles_t):
                    total = jnp.zeros((side, LANES), jnp.float32)
                    for code, turned in zip(codes, tiles):
                        total = jnp.where(code == 4 * q + fourth, turned, total)
                    first = (s * rp + r) * side
                    spread[h, to, first:first + side, q * LANES:(q + 1) * LANES] = total.astype(jnp.bfloat16)

    step_cols = 2 * LANES

    def multiply(h, d):
        left = at_all[:, partner(my_row, d, n_row)].reshape(group * side, sections * rp * side)
        for n in range(0, NCC * quarter, step_cols):
            part = jnp.dot(left, spread[h, d, :, n:n + step_cols], preferred_element_type=jnp.float32)
            part = part.reshape(group, side, step_cols)
            if d > 0:
                part = part + t_acc[h, :, :, n:n + step_cols]
            t_acc[h, :, :, n:n + step_cols] = part

    def turn_row(h, i):
        for q in range(tiles_t):
            tile = t_acc[h, i, :, q * LANES:(q + 1) * LANES]
            t_pick[h, i, q] = tile
            for k in range(1, 4):
                t_pick[h, i, k * tiles_t + q] = pltpu.roll(tile, k * quarter, axis=1)

    def pick(h, i, u):
        parts = []
        for g in range(4):
            c = c_cols[0, i, 4 * u + ORDER[g]]
            turn = lax.rem(g + 4 - lax.rem(c, 4), 4)
            parts.append(t_pick[h, i, turn * tiles_t + lax.div(c, 4)])
        return select4(lane, quarter, parts)

    def receive(h, d):
        if h == 0:
            code_copies[d - 1].wait_recv()
        p_copies[h][d - 1].wait_recv()
        spread_rows(h, partner(my_row, d, n_row), d)
        multiply(h, d)

    for h in range(2):
        spread_rows(h, my_row, 0)
    for copy in a_copies:
        copy.wait_recv()
    for h in range(2):
        multiply(h, 0)

    chained = n_layer == 4
    at_end = lax.rem(lax.div(my_layer + 1, 2), 2) == 0
    inside = jnp.logical_not(at_end)

    direct = [{}, {}]
    handed = []
    for h in range(2):
        for d in range(1, n_layer):
            direct[h][d] = pltpu.make_async_remote_copy(
                c_send.at[h, d - 1], c_recv.at[h, d - 1], zs.at[h, d - 1], zr.at[h, d - 1],
                device_id={"layer": partner(my_layer, d, n_layer)}, device_id_type=MESH)
        if chained:
            handed.append(pltpu.make_async_remote_copy(
                c_send.at[h, 2], via.at[h], vs.at[h], vr.at[h],
                device_id={"layer": partner(my_layer, 1, n_layer)}, device_id_type=MESH))

    def send(h, d):
        if not chained or d == 1:
            direct[h][d].start()
        elif d == 3:
            pl.when(at_end)(handed[h].start)
            pl.when(inside)(direct[h][3].start)
        else:
            pl.when(at_end)(direct[h][2].start)

    def hand_on(h):
        if chained:
            @pl.when(inside)
            def _():
                handed[h].wait_recv()
                c_send[h, 1] = (c_send[h, 1].astype(jnp.float32) + via[h].astype(jnp.float32)).astype(jnp.bfloat16)
                direct[h][2].start()

    for h in range(2):
        for d in range(1, n_row):
            receive(h, d)
            if h == 1 and d == n_row - 2:
                hand_on(0)
        for d in range(n_layer - 1, 0, -1):
            dst = partner(my_layer, d, n_layer)
            for o in range(own_rows):
                turn_row(h, dst * own_rows + o)
                for u in range(kc // 4):
                    c_send[h, d - 1, o, :, u * LANES:(u + 1) * LANES] = pick(
                        h, dst * own_rows + o, u).astype(jnp.bfloat16)
            send(h, d)
        for o in range(own_rows):
            turn_row(h, my_layer * own_rows + o)
            for u in range(kc // 4):
                own[h, o, :, u * LANES:(u + 1) * LANES] = pick(h, my_layer * own_rows + o, u)
    hand_on(1)

    def add(h, d):
        direct[h][d].wait_recv()
        own[h] = own[h] + c_recv[h, d - 1].astype(jnp.float32)

    for h in range(2):
        for d in range(1, n_layer):
            if chained and d == 3:
                pl.when(inside)(functools.partial(add, h, 3))
            else:
                add(h, d)
    for o in range(own_rows):
        for u in range(kc // 4):
            h0 = own[0, o, :, u * LANES:(u + 1) * LANES]
            h1 = own[1, o, :, u * LANES:(u + 1) * LANES]
            for e, tile in enumerate(pack(h0, h1, even, quarter)):
                at = (2 * u + e) * LANES
                out_ref[0, o, :, at:at + LANES] = tile.astype(jnp.bfloat16)
    for copy in sends:
        copy.wait_send()
    for h in range(2):
        for d in range(1, n_layer):
            if chained and d == 3:
                pl.when(at_end)(handed[h].wait_send)
                pl.when(inside)(direct[h][3].wait_send)
            else:
                direct[h][d].wait_send()


def local(dims, a_blocks, a_cols, p_blocks, p_cols, c_cols):
    n_row, n_col, n_layer = dims
    sections, rl, side, width = a_blocks.shape[1:]
    rp, p_width = p_blocks.shape[3], p_blocks.shape[5]
    group, kc = c_cols.shape[1:]
    own_rows = group // n_layer
    strip = (own_rows, side, kc * side)
    half_strip = (own_rows, side, kc * side // 2)
    depth = sections * rp * side
    dma = pltpu.SemaphoreType.DMA
    return pl.pallas_call(
        functools.partial(kernel, dims),
        out_shape=jax.ShapeDtypeStruct((1,) + strip, jnp.bfloat16),
        in_specs=[pl.BlockSpec(memory_space=pl.ANY)] * 5,
        out_specs=pl.BlockSpec(memory_space=pltpu.VMEM),
        scratch_shapes=[
            pltpu.SMEM(a_cols.shape, jnp.int32),
            pltpu.SMEM(p_cols.shape, jnp.int32),
            pltpu.SMEM(c_cols.shape, jnp.int32),
            pltpu.VMEM((sections, rl, side, width), jnp.bfloat16),
            pltpu.VMEM((sections, rp, side, p_width), jnp.bfloat16),
            pltpu.VMEM((2, n_row, sections, rp, side, LANES), jnp.bfloat16),
            pltpu.VMEM((n_row, sections * rp * 4, LANES), jnp.int32),
            pltpu.VMEM((n_col, n_row, rl * side, depth), jnp.bfloat16),
            pltpu.VMEM((2, n_row, depth, NCC * side // 2), jnp.bfloat16),
            pltpu.VMEM((2, group, side, NCC * side // 2), jnp.float32),
            pltpu.VMEM((2, group, NCC, side, LANES), jnp.float32),
            pltpu.VMEM((2,) + half_strip, jnp.float32),
            pltpu.VMEM((2, n_layer - 1) + half_strip, jnp.bfloat16),
            pltpu.VMEM((2, n_layer - 1) + half_strip, jnp.bfloat16),
            pltpu.VMEM((2,) + half_strip, jnp.bfloat16),
            dma((5,)),
            dma((2, n_row - 1)), dma((2, n_row - 1)),
            dma((n_row - 1,)), dma((n_row - 1,)),
            dma((n_col - 1,)), dma((n_col - 1,)),
            dma((2, n_layer - 1)), dma((2, n_layer - 1)),
            dma((2,)), dma((2,)),
        ],
        compiler_params=pltpu.CompilerParams(
            collective_id=0, has_side_effects=True, vmem_limit_bytes=63 * 2**20),
    )(a_blocks, a_cols, p_blocks, p_cols, c_cols)


def solution(mesh):
    dims = tuple(mesh.shape[x] for x in ("row", "col", "layer"))
    return jax.shard_map(
        functools.partial(local, dims),
        mesh=mesh,
        in_specs=(
            P("layer", None, ("row", "col"), None, None),
            P("layer", None, ("row", "col"), None),
            P("layer", None, "col", "row", None, None),
            P("layer", None, "col", "row", None),
            P("col", "row", None),
        ),
        out_specs=P("col", ("row", "layer"), None, None),
        check_vma=False,
    )
```

```python
import functools

import jax
import jax.numpy as jnp
from jax import lax
from jax.experimental import pallas as pl
from jax.experimental.pallas import tpu as pltpu
from jax.sharding import PartitionSpec as P

MESH = pl.DeviceIdType.MESH
LANES = 128
NCC = 16


def partner(me, d, n):
    out = 0
    bit = 1
    while bit < n:
        out = out + lax.rem(lax.div(me, bit) + ((d // bit) % 2), 2) * bit
        bit *= 2
    return out


def pair_codes(values, half):
    lane = lax.broadcasted_iota(jnp.int32, (1, LANES), 1)
    low = lane < half
    codes = []
    for p in range(len(values) // 2):
        codes.append(jnp.where(low, values[2 * p], values[2 * p + 1]))
        codes.append(jnp.where(low, values[2 * p + 1], values[2 * p]))
    return codes


def pair_tiles(x, half):
    tiles = []
    for p in range(x.shape[1] // LANES):
        tile = x[:, p * LANES:(p + 1) * LANES].astype(jnp.float32)
        tiles.append(tile)
        tiles.append(pltpu.roll(tile, half, axis=1))
    return tiles


def select4(lane, q, parts):
    out = parts[3]
    for g in (2, 1, 0):
        out = jnp.where(lane < (g + 1) * q, parts[g], out)
    return out


ORDER = (0, 2, 1, 3)


def pack(t0, t1, even, q):
    return jnp.where(even, t0, pltpu.roll(t1, q, axis=1)), jnp.where(even, pltpu.roll(t0, LANES - q, axis=1), t1)


def kernel(dims, a_hbm, a_cols_hbm, p_hbm, p_cols_hbm, c_cols_hbm, out_ref,
           a_cols, p_cols, c_cols, a_v, p_v, p_all, code_all, at_all, spread, t_acc, t_pick, own, c_send, c_recv,
           in_sem, ps, pr, cs, cr, as_, ar, zs, zr):
    n_row, n_col, n_layer = dims
    sections, rl, side, width = a_v.shape
    rp = p_all.shape[3]
    group = at_all.shape[0] * rl
    own_rows = c_send.shape[2]
    kc = c_cols.shape[2]
    quarter = side // 2
    tiles_t = NCC * quarter // LANES
    my_row, my_col, my_layer = (lax.axis_index(x) for x in ("row", "col", "layer"))

    barrier = pltpu.get_barrier_semaphore()
    for axis, me, n in (("row", my_row, n_row), ("col", my_col, n_col), ("layer", my_layer, n_layer)):
        for d in range(1, n):
            pl.semaphore_signal(barrier, inc=1, device_id={axis: partner(me, d, n)}, device_id_type=MESH)

    load_p = pltpu.make_async_copy(p_hbm.at[0, :, 0], p_v, in_sem.at[0])
    load_a = pltpu.make_async_copy(a_hbm.at[0], a_v, in_sem.at[1])
    load_pc = pltpu.make_async_copy(p_cols_hbm, p_cols, in_sem.at[2])
    load_ac = pltpu.make_async_copy(a_cols_hbm, a_cols, in_sem.at[3])
    load_cc = pltpu.make_async_copy(c_cols_hbm, c_cols, in_sem.at[4])
    for load in (load_p, load_pc, load_a, load_ac, load_cc):
        load.start()

    lane = lax.broadcasted_iota(jnp.int32, (side, LANES), 1)
    lane1 = lax.broadcasted_iota(jnp.int32, (1, LANES), 1)
    even = lax.rem(lax.div(lane, quarter), 2) == 0
    second = jnp.where(lane < side, 0, 1)
    fourth = lax.div(lane, quarter)

    load_pc.wait()
    for s in range(sections):
        for r in range(rp):
            cols = [p_cols[0, s, 0, r, j] for j in range(4)]
            for k in range(4):
                code = select4(lane1, quarter, [cols[ORDER[(g - k) % 4]] for g in range(4)])
                at = (s * rp + r) * 4 + k
                code_all[my_row, at:at + 1, :] = code
    load_p.wait()
    for s in range(sections):
        for r in range(rp):
            x = p_v[s, r].astype(jnp.float32)
            halves = pack(x[:, :LANES], x[:, LANES:], even, quarter)
            for h in range(2):
                p_all[h, my_row, s, r] = halves[h].astype(jnp.bfloat16)

    load_cc.wait()
    pl.semaphore_wait(barrier, (n_row - 1) + (n_col - 1) + (n_layer - 1))

    sends = []
    p_copies = [[], []]
    code_copies = []
    for d in range(1, n_row):
        to = {"row": partner(my_row, d, n_row)}
        code_copies.append(pltpu.make_async_remote_copy(
            code_all.at[my_row], code_all.at[my_row], cs.at[d - 1], cr.at[d - 1], device_id=to, device_id_type=MESH))
        for h in range(2):
            p_copies[h].append(pltpu.make_async_remote_copy(
                p_all.at[h, my_row], p_all.at[h, my_row], ps.at[h, d - 1], pr.at[h, d - 1],
                device_id=to, device_id_type=MESH))
    for copy in code_copies + p_copies[0] + p_copies[1]:
        copy.start()
        sends.append(copy)

    load_ac.wait()
    load_a.wait()
    for s in range(sections):
        for i in range(rl):
            codes = pair_codes([a_cols[0, s, i, k] for k in range(width // side)], side)
            codes = [jnp.broadcast_to(code, (side, LANES)) for code in codes]
            tiles = pair_tiles(a_v[s, i], side)
            for q in range(n_row * rp // 2):
                total = jnp.zeros((side, LANES), jnp.float32)
                for code, tile in zip(codes, tiles):
                    total = total + jnp.where(code == 2 * q + second, tile, 0.0)
                slot = 2 * q // rp
                start = (s * rp + 2 * q % rp) * side
                at_all[my_col, slot, i * side:(i + 1) * side, start:start + LANES] = total.astype(jnp.bfloat16)
    a_copies = []
    for d in range(1, n_col):
        copy = pltpu.make_async_remote_copy(
            at_all.at[my_col], at_all.at[my_col], as_.at[d - 1], ar.at[d - 1],
            device_id={"col": partner(my_col, d, n_col)}, device_id_type=MESH)
        copy.start()
        a_copies.append(copy)
        sends.append(copy)

    def spread_rows(h, slot, to):
        for s in range(sections):
            for r in range(rp):
                tile = p_all[h, slot, s, r].astype(jnp.float32)
                tiles = [tile] + [pltpu.roll(tile, k * quarter, axis=1) for k in range(1, 4)]
                codes = []
                for k in range(4):
                    at = (s * rp + r) * 4 + k
                    codes.append(jnp.broadcast_to(code_all[slot, at:at + 1, :], (side, LANES)))
                for q in range(tiles_t):
                    total = jnp.zeros((side, LANES), jnp.float32)
                    for code, turned in zip(codes, tiles):
                        total = jnp.where(code == 4 * q + fourth, turned, total)
                    first = (s * rp + r) * side
                    spread[h, to, first:first + side, q * LANES:(q + 1) * LANES] = total.astype(jnp.bfloat16)

    step_cols = 2 * LANES

    def multiply(h, d):
        left = at_all[:, partner(my_row, d, n_row)].reshape(group * side, sections * rp * side)
        for n in range(0, NCC * quarter, step_cols):
            part = jnp.dot(left, spread[h, d, :, n:n + step_cols], preferred_element_type=jnp.float32)
            part = part.reshape(group, side, step_cols)
            if d > 0:
                part = part + t_acc[h, :, :, n:n + step_cols]
            t_acc[h, :, :, n:n + step_cols] = part

    def turn_row(h, i):
        for q in range(tiles_t):
            tile = t_acc[h, i, :, q * LANES:(q + 1) * LANES]
            t_pick[h, i, q] = tile
            for k in range(1, 4):
                t_pick[h, i, k * tiles_t + q] = pltpu.roll(tile, k * quarter, axis=1)

    def pick(h, i, u):
        parts = []
        for g in range(4):
            c = c_cols[0, i, 4 * u + ORDER[g]]
            turn = lax.rem(g + 4 - lax.rem(c, 4), 4)
            parts.append(t_pick[h, i, turn * tiles_t + lax.div(c, 4)])
        return select4(lane, quarter, parts)

    def receive(h, d):
        if h == 0:
            code_copies[d - 1].wait_recv()
        p_copies[h][d - 1].wait_recv()
        spread_rows(h, partner(my_row, d, n_row), d)
        multiply(h, d)

    spread_rows(0, my_row, 0)
    for copy in a_copies:
        copy.wait_recv()
    multiply(0, 0)

    z_copies = [[], []]
    for h in range(2):
        if h == 1:
            spread_rows(1, my_row, 0)
            multiply(1, 0)
        for d in range(1, n_row):
            receive(h, d)
        for d in range(n_layer - 1, 0, -1):
            dst = partner(my_layer, d, n_layer)
            for o in range(own_rows):
                turn_row(h, dst * own_rows + o)
                for u in range(kc // 4):
                    c_send[h, d - 1, o, :, u * LANES:(u + 1) * LANES] = pick(
                        h, dst * own_rows + o, u).astype(jnp.bfloat16)
            copy = pltpu.make_async_remote_copy(
                c_send.at[h, d - 1], c_recv.at[h, d - 1], zs.at[h, d - 1], zr.at[h, d - 1],
                device_id={"layer": dst}, device_id_type=MESH)
            copy.start()
            z_copies[h].append(copy)
            sends.append(copy)
        for o in range(own_rows):
            turn_row(h, my_layer * own_rows + o)
            for u in range(kc // 4):
                own[h, o, :, u * LANES:(u + 1) * LANES] = pick(h, my_layer * own_rows + o, u)

    for h in range(2):
        for copy in z_copies[h]:
            copy.wait_recv()
        total = own[h]
        for d in range(1, n_layer):
            total = total + c_recv[h, d - 1].astype(jnp.float32)
        own[h] = total
    for o in range(own_rows):
        for u in range(kc // 4):
            h0 = own[0, o, :, u * LANES:(u + 1) * LANES]
            h1 = own[1, o, :, u * LANES:(u + 1) * LANES]
            for e, tile in enumerate(pack(h0, h1, even, quarter)):
                at = (2 * u + e) * LANES
                out_ref[0, o, :, at:at + LANES] = tile.astype(jnp.bfloat16)
    for copy in sends:
        copy.wait_send()


def local(dims, a_blocks, a_cols, p_blocks, p_cols, c_cols):
    n_row, n_col, n_layer = dims
    sections, rl, side, width = a_blocks.shape[1:]
    rp, p_width = p_blocks.shape[3], p_blocks.shape[5]
    group, kc = c_cols.shape[1:]
    own_rows = group // n_layer
    strip = (own_rows, side, kc * side)
    half_strip = (own_rows, side, kc * side // 2)
    depth = sections * rp * side
    dma = pltpu.SemaphoreType.DMA
    return pl.pallas_call(
        functools.partial(kernel, dims),
        out_shape=jax.ShapeDtypeStruct((1,) + strip, jnp.bfloat16),
        in_specs=[pl.BlockSpec(memory_space=pl.ANY)] * 5,
        out_specs=pl.BlockSpec(memory_space=pltpu.VMEM),
        scratch_shapes=[
            pltpu.SMEM(a_cols.shape, jnp.int32),
            pltpu.SMEM(p_cols.shape, jnp.int32),
            pltpu.SMEM(c_cols.shape, jnp.int32),
            pltpu.VMEM((sections, rl, side, width), jnp.bfloat16),
            pltpu.VMEM((sections, rp, side, p_width), jnp.bfloat16),
            pltpu.VMEM((2, n_row, sections, rp, side, LANES), jnp.bfloat16),
            pltpu.VMEM((n_row, sections * rp * 4, LANES), jnp.int32),
            pltpu.VMEM((n_col, n_row, rl * side, depth), jnp.bfloat16),
            pltpu.VMEM((2, n_row, depth, NCC * side // 2), jnp.bfloat16),
            pltpu.VMEM((2, group, side, NCC * side // 2), jnp.float32),
            pltpu.VMEM((2, group, NCC, side, LANES), jnp.float32),
            pltpu.VMEM((2,) + half_strip, jnp.float32),
            pltpu.VMEM((2, n_layer - 1) + half_strip, jnp.bfloat16),
            pltpu.VMEM((2, n_layer - 1) + half_strip, jnp.bfloat16),
            dma((5,)),
            dma((2, n_row - 1)), dma((2, n_row - 1)),
            dma((n_row - 1,)), dma((n_row - 1,)),
            dma((n_col - 1,)), dma((n_col - 1,)),
            dma((2, n_layer - 1)), dma((2, n_layer - 1)),
        ],
        compiler_params=pltpu.CompilerParams(
            collective_id=0, has_side_effects=True, vmem_limit_bytes=63 * 2**20),
    )(a_blocks, a_cols, p_blocks, p_cols, c_cols)


def solution(mesh):
    dims = tuple(mesh.shape[x] for x in ("row", "col", "layer"))
    return jax.shard_map(
        functools.partial(local, dims),
        mesh=mesh,
        in_specs=(
            P("layer", None, ("row", "col"), None, None),
            P("layer", None, ("row", "col"), None),
            P("layer", None, "col", "row", None, None),
            P("layer", None, "col", "row", None),
            P("col", "row", None),
        ),
        out_specs=P("col", ("row", "layer"), None, None),
        check_vma=False,
    )
```
